32 devices in a mesh: groups: 2 (over y), expert: 4 (over x, core), fsdp: 4 (over z).
Axes of the slice: x: 2, y: 2, z: 4, core: 2. Of those that a mesh axis runs over, the one named last changes fastest.
Arguments:
- tokens: bfloat16 [32768, 512], P(('groups', 'expert', 'fsdp')), parts along dimension 0, may hold values from -6 to 6
- routes: int32 [32768], P(('groups', 'expert', 'fsdp')), parts along dimension 0, may hold values from 0 to 7, as said below
- slot_ids: int32 [32768], P(('groups', 'expert', 'fsdp')), parts along dimension 0, may hold values from 0 to 159, as said below
- qkv_weight: bfloat16 [512, 1536], P('fsdp'), may hold values from -0.25 to 0.25
- proj_weight: bfloat16 [512, 512], P('fsdp'), may hold values from -0.25 to 0.25
- logit_scale: float32 [16], replicated, may hold values from 1.5 to 5.5
- bias_network_first_weight: float32 [2, 512], P(None, 'fsdp'), may hold values from -4 to 4
- bias_network_first_offset: float32 [512], P('fsdp'), may hold values from -3 to 3
- bias_network_second_weight: float32 [512, 16], P('fsdp'), may hold values from -0.25 to 0.25
- attn_gain: float32 [512], replicated, may hold values from 0.1 to 1.9
- router: bfloat16 [512, 8], replicated, may hold values from -0.25 to 0.25
- moe_gain: float32 [512], replicated, may hold values from 0.1 to 1.9
- expert_in: bfloat16 [8, 512, 2048], P('expert'), may hold values from -0.25 to 0.25
- expert_out: bfloat16 [8, 2048, 512], P('expert'), may hold values from -0.125 to 0.125
Outputs:
- block_out: bfloat16 [32768, 512], P(('groups', 'expert', 'fsdp')), parts along dimension 0
The draws below stay inside these ranges and needn't reach their ends.
There are 2 independent parts, one for each index of `groups`. The reference program is written for one: setup_inputs(seed, part) draws one part's arguments, and reference() takes and returns one part's arrays. A program takes and returns all parts, laid end to end along the dimension named above; an argument that names none is the same for every part. Nothing has to cross between parts.
Inputs may be any that keep to these rules, and one draw needn't show every extreme that they name: `routes`: each device's 1024 tokens name every expert at most 160 times; one expert, the same on every device, is named exactly 160 times by each device's tokens. `slot_ids`: among one device's tokens with the same route, the slots are distinct.
All inputs are finite; a program needn't handle non-finite values.
Results may differ from the reference program's by a relative error of at most 0.012.
The reference program's roundings to bfloat16 on the way count: a program that leaves them out, or rounds other values in their place, can miss the bound.
Values may be sent and summed in bfloat16 or wider, within the bound.
A program may use at most 192 MiB of HBM per device.

```python
import math
import jax
import jax.numpy as jnp
from jax import lax

D = 512
ATTENTION_HEADS = 16
WIN = 16
POSITION_HIDDEN = 512
FF = 2048
TOK_DEV = 1024
EXPERTS = 8
CAP = 160
TOKENS = 16384


def route_table(base_key):
    bias_table_random_key = jax.random.fold_in(base_key, 11)
    slot_total = EXPERTS * CAP
    device_count = TOKENS // TOK_DEV
    filled = jax.random.randint(jax.random.fold_in(bias_table_random_key, 1), (), 0, EXPERTS)
    device_keys = jax.random.split(jax.random.fold_in(bias_table_random_key, 2), device_count)
    owners = jnp.arange(slot_total, dtype=jnp.int32) // CAP

    def one_device(device_key):
        order_key, mixing_key = jax.random.split(device_key)
        ranking = jnp.argsort(jax.random.permutation(order_key, slot_total)).astype(jnp.int32)
        ordering = jnp.where(owners == filled, ranking - slot_total, ranking)
        chosen = jnp.argsort(ordering)[:TOK_DEV].astype(jnp.int32)
        return chosen[jax.random.permutation(mixing_key, TOK_DEV)]
    return jax.vmap(one_device)(device_keys).reshape(TOKENS).astype(jnp.int32)


def draw_routes(key, part):
    return route_table(key) // CAP


def draw_slot_ids(key, part):
    return route_table(key) % CAP


def shard_levels(rng, shape, cuts, smallest, top_value):
    gain = 1.0
    for axis_at, blocks in cuts:
        heights = jax.random.uniform(jax.random.fold_in(jax.random.fold_in(rng, 6), axis_at), (blocks,), jnp.float32, smallest / len(cuts), top_value / len(cuts))
        gain = gain * jnp.repeat(jnp.exp(heights), shape[axis_at] // blocks).reshape((-1,) + (1,) * (len(shape) - 1 - axis_at))
    return gain


def gaussian(rng, extent, scale, bound, cuts=(), kind=jnp.bfloat16):
    level = shard_levels(rng, extent, cuts, -0.22, 0.18) if cuts else 1.0
    entries = jax.random.normal(rng, extent, jnp.float32) * scale * level
    return jnp.minimum(jnp.maximum(entries, -bound), bound).astype(kind)


def setup_inputs(seed: int = 0, part: int = 0) -> dict:
    seeds = jax.random.split(jax.random.key(seed), 15)
    part_keys = jax.random.split(jax.random.fold_in(seeds[14], part), 15)
    tokens = gaussian(part_keys[0], (TOKENS, D), 1.0, 6.0, ((0, 16),))
    routes = draw_routes(jax.random.fold_in(jax.random.fold_in(seeds[14], part), 71), part)
    slot_ids = draw_slot_ids(jax.random.fold_in(jax.random.fold_in(seeds[14], part), 71), part)
    qkv_weight = gaussian(seeds[3], (D, 3 * D), D ** -0.5, 0.25, ((0, 4),))
    proj_weight = gaussian(seeds[4], (D, D), D ** -0.5, 0.25, ((0, 4),))
    logit_scale = jnp.clip(jax.random.uniform(seeds[5], (ATTENTION_HEADS,), jnp.float32, 1.5, 5.5), 1.5, 5.5)
    bias_network_first_weight = gaussian(seeds[6], (2, POSITION_HIDDEN), 2 ** -0.5, 4.0, ((1, 4),), jnp.float32)
    bias_network_first_offset = gaussian(seeds[7], (POSITION_HIDDEN,), 0.5, 3.0, ((0, 4),), jnp.float32)
    bias_network_second_weight = gaussian(seeds[8], (POSITION_HIDDEN, ATTENTION_HEADS), POSITION_HIDDEN ** -0.5, 0.25, ((0, 4),), jnp.float32)
    attn_gain = jnp.clip(1.0 + 0.18 * jax.random.normal(seeds[9], (D,), jnp.float32), 0.1, 1.9)
    router = gaussian(seeds[10], (D, EXPERTS), D ** -0.5, 0.25)
    moe_gain = jnp.clip(1.0 + 0.18 * jax.random.normal(seeds[11], (D,), jnp.float32), 0.1, 1.9)
    expert_in = gaussian(seeds[12], (EXPERTS, D, FF), D ** -0.5, 0.25, ((0, 4),))
    expert_out = gaussian(seeds[13], (EXPERTS, FF, D), FF ** -0.5, 0.125, ((0, 4),))
    return dict(tokens=tokens, routes=routes, slot_ids=slot_ids, qkv_weight=qkv_weight, proj_weight=proj_weight, logit_scale=logit_scale, bias_network_first_weight=bias_network_first_weight, bias_network_first_offset=bias_network_first_offset, bias_network_second_weight=bias_network_second_weight, attn_gain=attn_gain, router=router, moe_gain=moe_gain, expert_in=expert_in, expert_out=expert_out)


norm_eps = 1e-05
unit_eps = 1e-06
highest = lax.Precision.HIGHEST

def relative_coords(window):
    span_size = 2 * window - 1
    offsets = jnp.arange(span_size, dtype=jnp.float32) - (window - 1)
    log_stretched_coords = offsets / max(window - 1, 1) * 8.0
    logged = jnp.sign(log_stretched_coords) * jnp.log2(jnp.abs(log_stretched_coords) + 1.0) / 3.0
    return jnp.stack([jnp.repeat(logged, span_size), jnp.tile(logged, span_size)], axis=1)

def layer_norm(values, gain_vector):
    centre = values - lax.optimization_barrier(jnp.mean(values, axis=-1, keepdims=True))
    spread = lax.optimization_barrier(jnp.mean(centre * centre, axis=-1, keepdims=True))
    return centre * lax.rsqrt(spread + norm_eps) * gain_vector

def unit_rows(values):
    return values * lax.rsqrt(lax.optimization_barrier(jnp.sum(values * values, axis=-1, keepdims=True)) + unit_eps)

def as_wide(values):
    return lax.optimization_barrier(values.astype(jnp.bfloat16)).astype(jnp.float32)

def window_attention(qkv_rows, head_scale, rel_bias, head_count, window_tokens):
    total_rows, triple = qkv_rows.shape
    width = triple // 3
    windows = total_rows // window_tokens
    split_up = qkv_rows.reshape(windows, window_tokens, 3, head_count, width // head_count)
    unit_query = as_wide(unit_rows(split_up[:, :, 0]))
    unit_key = as_wide(unit_rows(split_up[:, :, 1]))
    value_rows = as_wide(split_up[:, :, 2])
    scores = jnp.einsum('wqhd,wkhd->whqk', unit_query, unit_key)
    scores = scores * head_scale[None, :, None, None] + rel_bias[None]
    shifted = jnp.exp(scores - lax.optimization_barrier(jnp.max(scores, axis=-1, keepdims=True)))
    weights = as_wide(shifted / lax.optimization_barrier(jnp.sum(shifted, axis=-1, keepdims=True)))
    context = jnp.einsum('whqk,wkhd->wqhd', weights, value_rows)
    return context.astype(jnp.bfloat16).reshape(total_rows, width)

def reference(tokens, routes, slot_ids, qkv_weight, proj_weight, logit_scale, bias_network_first_weight, bias_network_first_offset, bias_network_second_weight, attn_gain, router, moe_gain, expert_in, expert_out):
    coords = relative_coords(WIN)
    bias_hidden = jax.nn.relu(jnp.dot(coords, bias_network_first_weight, precision=highest) + bias_network_first_offset)
    bias_table = 16.0 * jax.nn.sigmoid(jnp.dot(bias_hidden, bias_network_second_weight, precision=highest))
    span_size = 2 * WIN - 1
    positions = jnp.arange(WIN * WIN, dtype=jnp.int32)
    row_of = positions // WIN
    column_of = positions % WIN
    lookup = (row_of[:, None] - row_of[None, :] + WIN - 1) * span_size + (column_of[:, None] - column_of[None, :] + WIN - 1)
    rel_bias = jnp.take(bias_table.T, lookup.astype(jnp.int32), axis=1)
    head_scale = jnp.exp(jnp.minimum(logit_scale, math.log(100.0)))
    device_count = TOKENS // TOK_DEV

    def attention_part(token_rows):
        qkv = jnp.dot(token_rows, qkv_weight, preferred_element_type=jnp.float32)
        context = window_attention(qkv, head_scale, rel_bias, ATTENTION_HEADS, WIN * WIN)
        attended = jnp.dot(context, proj_weight, preferred_element_type=jnp.float32)
        return token_rows.astype(jnp.float32) + layer_norm(attended, attn_gain)
    residual = lax.map(attention_part, tokens.reshape(device_count, TOK_DEV, D)).reshape(TOKENS, D)
    normed = layer_norm(residual, moe_gain).astype(jnp.bfloat16)
    logits = jnp.dot(normed, router, preferred_element_type=jnp.float32)
    gate = jax.nn.sigmoid(jnp.take_along_axis(logits, routes[:, None].astype(jnp.int32), axis=1)[:, 0])
    owner_device = jnp.arange(TOKENS, dtype=jnp.int32) // TOK_DEV
    slot_index = ((owner_device * EXPERTS + routes) * CAP + slot_ids).astype(jnp.int32)
    buffer = jnp.zeros((device_count * EXPERTS * CAP, D), jnp.bfloat16).at[slot_index].set(normed)
    buffer = buffer.reshape(device_count, EXPERTS, CAP, D).transpose(1, 0, 2, 3).reshape(EXPERTS, device_count * CAP, D)

    def one_expert(items):
        rows_in, first_weight, second_weight = items
        inner = jnp.dot(rows_in, first_weight, preferred_element_type=jnp.float32)
        inner = jax.nn.gelu(inner, approximate=False).astype(jnp.bfloat16)
        return jnp.dot(inner, second_weight, preferred_element_type=jnp.float32).astype(jnp.bfloat16)
    answers = lax.map(one_expert, (buffer, expert_in, expert_out))
    answers = answers.reshape(EXPERTS, device_count, CAP, D).transpose(1, 0, 2, 3).reshape(device_count * EXPERTS * CAP, D)
    picked = jnp.take(answers, slot_index, axis=0).astype(jnp.float32)
    return (residual + gate[:, None] * picked).astype(jnp.bfloat16)
```

```python
import functools
import math

import jax
import jax.numpy as jnp
import numpy as np
from jax import lax
from jax.experimental import pallas as pl
from jax.experimental.pallas import tpu as pltpu
from jax.sharding import PartitionSpec as P

HEADS = 16
WIN = 16
WTOK = WIN * WIN
LOG2E = math.log2(math.e)
NORM_EPS = 1e-05
UNIT_EPS = 1e-06
HIGHEST = lax.Precision.HIGHEST
MIB = 1024 * 1024
F32 = jnp.float32
BF16 = jnp.bfloat16


def table_coords():
    offsets = (WIN - 1 - np.arange(32)).astype(np.float32)
    stretched = offsets / np.float32(WIN - 1) * np.float32(8.0)
    logged = np.sign(stretched) * np.log2(np.abs(stretched) + np.float32(1.0)) / np.float32(3.0)
    logged = logged.astype(np.float32)
    out = np.zeros((1024, 8), np.float32)
    out[:, 0] = np.repeat(logged, 32)
    out[:, 1] = np.tile(logged, 32)
    return out


def layer_norm(values, gain):
    centre = values - jnp.mean(values, axis=-1, keepdims=True)
    spread = jnp.mean(centre * centre, axis=-1, keepdims=True)
    return centre * lax.rsqrt(spread + NORM_EPS) * gain


def dot(a, b):
    return jnp.dot(a, b, preferred_element_type=F32)


def dot_nt(a, b, precision=None):
    return lax.dot_general(
        a, b, (((1,), (1,)), ((), ())), precision=precision, preferred_element_type=F32
    )


def build_bias(net_ref, coords_ref, strips, bias):
    shard_count = net_ref.shape[0]
    c0 = coords_ref[:, 0:1]
    c1 = coords_ref[:, 1:2]
    table = None
    for z in range(shard_count):
        hidden = c0 * net_ref[z, 16:17, :] + c1 * net_ref[z, 17:18, :] + net_ref[z, 18:19, :]
        hidden = jnp.maximum(hidden, 0.0)
        part = dot_nt(net_ref[z, 0:16, :], hidden, HIGHEST)
        table = part if table is None else table + part
    table = (16.0 * LOG2E) * jax.nn.sigmoid(table)
    stacked = jnp.concatenate([table[:, g * 256 : (g + 1) * 256] for g in range(4)], axis=0)
    high = stacked.astype(BF16)
    rest = stacked - high.astype(F32)
    mid = rest.astype(BF16)
    low = (rest - mid.astype(F32)).astype(BF16)
    pieces = jnp.concatenate([high, mid, low], axis=0)
    k = lax.broadcasted_iota(jnp.int32, (256, 128), 0)
    c = lax.broadcasted_iota(jnp.int32, (256, 128), 1)
    same_row = (k // 32) == (c // 16)
    shift = (k % 32) - (c % 16)
    for xi in range(16):
        sel = jnp.where(same_row & (shift == 15 - xi), 1.0, 0.0).astype(BF16)
        picked = dot(pieces, sel)
        strips[xi] = picked[0:64] + picked[64:128] + picked[128:192]
    for h in range(HEADS):
        strip = jnp.concatenate([strips[:, g * 16 + h, :] for g in range(4)], axis=1)
        for yi in range(16):
            start = (15 - yi) * 16
            bias[h, yi * 16 : (yi + 1) * 16, :] = strip[:, start : start + 256]


def attention_kernel(
    tok_ref, wqkv_ref, wproj_ref, net_ref, coords_ref, ls_ref, ag_ref, mg_ref,
    res_ref, normed_ref, strips, bias, ones_ref, ctx_ref,
):
    @pl.when(pl.program_id(0) == 0)
    def _():
        build_bias(net_ref, coords_ref, strips, bias)
        r = lax.broadcasted_iota(jnp.int32, ones_ref.shape, 0)
        c = lax.broadcasted_iota(jnp.int32, ones_ref.shape, 1)
        ones_ref[...] = jnp.where((r // 32) == (c // 32), 1.0, 0.0).astype(BF16)

    width = tok_ref.shape[1]
    tok = tok_ref[...]
    scales = jnp.exp(jnp.minimum(ls_ref[...], math.log(100.0))) * LOG2E
    lane = lax.broadcasted_iota(jnp.int32, (WTOK, 128), 1) // 32

    def unit(col):
        x = dot(tok, wqkv_ref[:, col : col + 256])
        sq = x * x
        high = sq.astype(BF16)
        low = (sq - high.astype(F32)).astype(BF16)
        ones = ones_ref[...]
        total = dot(high, ones) + dot(low, ones)
        return (x * lax.rsqrt(total + UNIT_EPS)).astype(BF16)

    for pair in range(width // 256):
        base = pair * 256
        uq2 = unit(base)
        uk2 = unit(width + base)
        v2 = dot(tok, wqkv_ref[:, 2 * width + base : 2 * width + base + 256]).astype(BF16)
        for half in range(2):
            uq = uq2[:, half * 128 : (half + 1) * 128]
            uk = uk2[:, half * 128 : (half + 1) * 128]
            v = v2[:, half * 128 : (half + 1) * 128]
            ctx = None
            for j in range(4):
                h = pair * 8 + half * 4 + j
                q = jnp.where(lane == j, uq, jnp.zeros_like(uq))
                s = dot_nt(q, uk) * scales[:, h : h + 1] + bias[h]
                e = jnp.exp2(s - jnp.max(s, axis=-1, keepdims=True))
                w = (e * (1.0 / jnp.sum(e, axis=-1, keepdims=True))).astype(BF16)
                o = dot(w, v)
                ctx = o if ctx is None else jnp.where(lane == j, o, ctx)
            ctx_ref[:, base + half * 128 : base + (half + 1) * 128] = ctx.astype(BF16)

    attended = dot(ctx_ref[...], wproj_ref[...])
    residual = tok.astype(F32) + layer_norm(attended, ag_ref[...])
    res_ref[...] = residual
    normed_ref[...] = layer_norm(residual, mg_ref[...]).astype(BF16)


def whole_block(shape):
    return pl.BlockSpec(shape, lambda i: (0,) * len(shape))


def attention(tokens, wqkv, wproj, net, logit_scale, attn_gain, moe_gain):
    rows, width = tokens.shape
    coords = jnp.asarray(table_coords())
    rows_block = pl.BlockSpec((WTOK, width), lambda i: (i, 0))
    return pl.pallas_call(
        attention_kernel,
        grid=(rows // WTOK,),
        out_shape=(
            jax.ShapeDtypeStruct((rows, width), F32),
            jax.ShapeDtypeStruct((rows, width), BF16),
        ),
        in_specs=[
            rows_block,
            whole_block(wqkv.shape),
            whole_block(wproj.shape),
            whole_block(net.shape),
            whole_block(coords.shape),
            whole_block((1, HEADS)),
            whole_block((1, width)),
            whole_block((1, width)),
        ],
        out_specs=(rows_block, rows_block),
        scratch_shapes=[
            pltpu.VMEM((16, 64, 128), F32),
            pltpu.VMEM((HEADS, WTOK, WTOK), F32),
            pltpu.VMEM((256, 256), BF16),
            pltpu.VMEM((WTOK, width), BF16),
        ],
        compiler_params=pltpu.CompilerParams(vmem_limit_bytes=48 * MIB),
        name="attention",
    )(
        tokens, wqkv, wproj, net, coords, logit_scale.reshape(1, HEADS),
        attn_gain.reshape(1, width), moe_gain.reshape(1, width),
    )


def combine_kernel(cap, res_ref, normed_ref, router_ref, routes_ref, slots_ref, ret_ref, out_ref):
    rows = res_ref.shape[0]
    slots = ret_ref.shape[0]
    eye = lax.broadcasted_iota(jnp.int32, (rows, rows), 0) == lax.broadcasted_iota(
        jnp.int32, (rows, rows), 1
    )

    def column(row):
        wide = jnp.where(eye, row.astype(F32), 0.0)
        return jnp.sum(wide, axis=1, keepdims=True).astype(jnp.int32)

    routes = column(routes_ref[...])
    place = column(routes_ref[...] * cap + slots_ref[...])
    logits = dot(normed_ref[...], router_ref[...])
    expert = lax.broadcasted_iota(jnp.int32, logits.shape, 1)
    picked = jnp.sum(jnp.where(expert == routes, logits, 0.0), axis=1, keepdims=True)
    gate = jax.nn.sigmoid(picked)
    spot = lax.broadcasted_iota(jnp.int32, (rows, slots), 1)
    one_hot = jnp.where(spot == place, 1.0, 0.0).astype(BF16)
    out_ref[...] = (res_ref[...] + gate * dot(one_hot, ret_ref[...])).astype(BF16)


def combine(residual, normed, router, routes, slot_ids, returned, cap):
    rows, width = residual.shape
    step = WTOK
    rows_block = pl.BlockSpec((step, width), lambda i: (i, 0))
    ids_block = pl.BlockSpec((1, step), lambda i: (0, i))
    return pl.pallas_call(
        functools.partial(combine_kernel, cap),
        grid=(rows // step,),
        out_shape=jax.ShapeDtypeStruct((rows, width), BF16),
        in_specs=[
            rows_block, rows_block, whole_block(router.shape), ids_block, ids_block,
            whole_block(returned.shape),
        ],
        out_specs=rows_block,
        compiler_params=pltpu.CompilerParams(vmem_limit_bytes=48 * MIB),
        name="combine",
    )(residual, normed, router, routes.reshape(1, rows), slot_ids.reshape(1, rows), returned)


def run_experts(arrived, first_weight, second_weight):
    inner = jnp.einsum("secd,edf->secf", arrived, first_weight, preferred_element_type=F32)
    inner = jax.nn.gelu(inner, approximate=False).astype(BF16)
    return jnp.einsum("secf,efd->secd", inner, second_weight, preferred_element_type=F32).astype(BF16)


def shards(
    tokens, routes, slot_ids, qkv_weight, proj_weight, logit_scale, first_weight, first_offset,
    second_weight, attn_gain, router, moe_gain, expert_in, expert_out,
):
    rows, width = tokens.shape
    units = first_weight.shape[1]
    net = jnp.concatenate(
        [second_weight.T, first_weight, first_offset[None], jnp.zeros((5, units), F32)], axis=0
    )
    net = lax.all_gather(net, "fsdp", axis=0)
    wqkv = lax.all_gather(qkv_weight, "fsdp", axis=0, tiled=True)
    wproj = lax.all_gather(proj_weight, "fsdp", axis=0, tiled=True)
    residual, normed = attention(tokens, wqkv, wproj, net, logit_scale, attn_gain, moe_gain)
    experts = router.shape[1]
    held = expert_in.shape[0]
    ranks = lax.axis_size("expert")
    cap = rows * 5 // (4 * experts)
    column = routes * cap + slot_ids
    one_hot = (column[:, None] == jnp.arange(experts * cap, dtype=jnp.int32)[None, :]).astype(BF16)
    packed = lax.dot_general(
        one_hot, normed, (((0,), (0,)), ((), ())), preferred_element_type=F32
    ).astype(BF16)
    arrived = lax.all_to_all(
        packed.reshape(ranks, held, cap, width), "expert", split_axis=0, concat_axis=0, tiled=True
    )
    answers = run_experts(arrived, expert_in, expert_out)
    returned = lax.all_to_all(answers, "expert", split_axis=0, concat_axis=0, tiled=True)
    returned = returned.reshape(experts * cap, width)
    return combine(residual, normed, router, routes, slot_ids, returned, cap)


def solution(mesh):
    rows = P(("groups", "expert", "fsdp"))
    return jax.shard_map(
        shards,
        mesh=mesh,
        in_specs=(
            P(("groups", "expert", "fsdp"), None), rows, rows, P("fsdp", None), P("fsdp", None),
            P(), P(None, "fsdp"), P("fsdp"), P("fsdp", None), P(), P(), P(),
            P("expert", None, None), P("expert", None, None),
        ),
        out_specs=P(("groups", "expert", "fsdp"), None),
        check_vma=False,
    )
```

```python
import functools
import math

import jax
import jax.numpy as jnp
import numpy as np
from jax import lax
from jax.experimental import pallas as pl
from jax.experimental.pallas import tpu as pltpu
from jax.sharding import PartitionSpec as P

HEADS = 16
WIN = 16
WTOK = WIN * WIN
LOG2E = math.log2(math.e)
NORM_EPS = 1e-05
UNIT_EPS = 1e-06
HIGHEST = lax.Precision.HIGHEST
MIB = 1024 * 1024
F32 = jnp.float32
BF16 = jnp.bfloat16


def table_coords():
    offsets = (WIN - 1 - np.arange(32)).astype(np.float32)
    stretched = offsets / np.float32(WIN - 1) * np.float32(8.0)
    logged = np.sign(stretched) * np.log2(np.abs(stretched) + np.float32(1.0)) / np.float32(3.0)
    logged = logged.astype(np.float32)
    out = np.zeros((1024, 8), np.float32)
    out[:, 0] = np.repeat(logged, 32)
    out[:, 1] = np.tile(logged, 32)
    return out


def layer_norm(values, gain):
    centre = values - jnp.mean(values, axis=-1, keepdims=True)
    spread = jnp.mean(centre * centre, axis=-1, keepdims=True)
    return centre * lax.rsqrt(spread + NORM_EPS) * gain


def dot(a, b):
    return jnp.dot(a, b, preferred_element_type=F32)


def dot_nt(a, b, precision=None):
    return lax.dot_general(
        a, b, (((1,), (1,)), ((), ())), precision=precision, preferred_element_type=F32
    )


def build_bias(net_ref, coords_ref, strips, bias):
    shard_count = net_ref.shape[0]
    c0 = coords_ref[:, 0:1]
    c1 = coords_ref[:, 1:2]
    table = None
    for z in range(shard_count):
        hidden = c0 * net_ref[z, 16:17, :] + c1 * net_ref[z, 17:18, :] + net_ref[z, 18:19, :]
        hidden = jnp.maximum(hidden, 0.0)
        part = dot_nt(net_ref[z, 0:16, :], hidden, HIGHEST)
        table = part if table is None else table + part
    table = (16.0 * LOG2E) * jax.nn.sigmoid(table)
    stacked = jnp.concatenate([table[:, g * 256 : (g + 1) * 256] for g in range(4)], axis=0)
    high = stacked.astype(BF16)
    rest = stacked - high.astype(F32)
    mid = rest.astype(BF16)
    low = (rest - mid.astype(F32)).astype(BF16)
    pieces = jnp.concatenate([high, mid, low], axis=0)
    k = lax.broadcasted_iota(jnp.int32, (256, 128), 0)
    c = lax.broadcasted_iota(jnp.int32, (256, 128), 1)
    same_row = (k // 32) == (c // 16)
    shift = (k % 32) - (c % 16)
    for xi in range(16):
        sel = jnp.where(same_row & (shift == 15 - xi), 1.0, 0.0).astype(BF16)
        picked = dot(pieces, sel)
        strips[xi] = picked[0:64] + picked[64:128] + picked[128:192]
    for h in range(HEADS):
        strip = jnp.concatenate([strips[:, g * 16 + h, :] for g in range(4)], axis=1)
        for yi in range(16):
            start = (15 - yi) * 16
            bias[h, yi * 16 : (yi + 1) * 16, :] = strip[:, start : start + 256]


def attention_kernel(
    tok_ref, wqkv_ref, wproj_ref, net_ref, coords_ref, ls_ref, ag_ref, mg_ref,
    res_ref, normed_ref, strips, bias, ones_ref, ctx_ref,
):
    @pl.when(pl.program_id(0) == 0)
    def _():
        build_bias(net_ref, coords_ref, strips, bias)
        r = lax.broadcasted_iota(jnp.int32, ones_ref.shape, 0)
        c = lax.broadcasted_iota(jnp.int32, ones_ref.shape, 1)
        ones_ref[...] = jnp.where((r // 32) == (c // 32), 1.0, 0.0).astype(BF16)

    width = tok_ref.shape[1]
    tok = tok_ref[...]
    scales = jnp.exp(jnp.minimum(ls_ref[...], math.log(100.0))) * LOG2E
    lane = lax.broadcasted_iota(jnp.int32, (WTOK, 128), 1) // 32

    def unit(col):
        x = dot(tok, wqkv_ref[:, col : col + 256])
        sq = x * x
        high = sq.astype(BF16)
        low = (sq - high.astype(F32)).astype(BF16)
        ones = ones_ref[...]
        total = dot(high, ones) + dot(low, ones)
        return (x * lax.rsqrt(total + UNIT_EPS)).astype(BF16)

    for pair in range(width // 256):
        base = pair * 256
        uq2 = unit(base)
        uk2 = unit(width + base)
        v2 = dot(tok, wqkv_ref[:, 2 * width + base : 2 * width + base + 256]).astype(BF16)
        for half in range(2):
            uq = uq2[:, half * 128 : (half + 1) * 128]
            uk = uk2[:, half * 128 : (half + 1) * 128]
            v = v2[:, half * 128 : (half + 1) * 128]
            ctx = None
            for j in range(4):
                h = pair * 8 + half * 4 + j
                q = jnp.where(lane == j, uq, jnp.zeros_like(uq))
                s = dot_nt(q, uk) * scales[:, h : h + 1] + bias[h]
                e = jnp.exp2(s - jnp.max(s, axis=-1, keepdims=True))
                w = (e * (1.0 / jnp.sum(e, axis=-1, keepdims=True))).astype(BF16)
                o = dot(w, v)
                ctx = o if ctx is None else jnp.where(lane == j, o, ctx)
            ctx_ref[:, base + half * 128 : base + (half + 1) * 128] = ctx.astype(BF16)

    attended = dot(ctx_ref[...], wproj_ref[...])
    residual = tok.astype(F32) + layer_norm(attended, ag_ref[...])
    res_ref[...] = residual
    normed_ref[...] = layer_norm(residual, mg_ref[...]).astype(BF16)


def whole_block(shape):
    return pl.BlockSpec(shape, lambda i: (0,) * len(shape))


def attention(tokens, wqkv, wproj, net, logit_scale, attn_gain, moe_gain):
    rows, width = tokens.shape
    coords = jnp.asarray(table_coords())
    rows_block = pl.BlockSpec((WTOK, width), lambda i: (i, 0))
    return pl.pallas_call(
        attention_kernel,
        grid=(rows // WTOK,),
        out_shape=(
            jax.ShapeDtypeStruct((rows, width), F32),
            jax.ShapeDtypeStruct((rows, width), BF16),
        ),
        in_specs=[
            rows_block,
            whole_block(wqkv.shape),
            whole_block(wproj.shape),
            whole_block(net.shape),
            whole_block(coords.shape),
            whole_block((1, HEADS)),
            whole_block((1, width)),
            whole_block((1, width)),
        ],
        out_specs=(rows_block, rows_block),
        scratch_shapes=[
            pltpu.VMEM((16, 64, 128), F32),
            pltpu.VMEM((HEADS, WTOK, WTOK), F32),
            pltpu.VMEM((256, 256), BF16),
            pltpu.VMEM((WTOK, width), BF16),
        ],
        compiler_params=pltpu.CompilerParams(vmem_limit_bytes=48 * MIB),
        name="attention",
    )(
        tokens, wqkv, wproj, net, coords, logit_scale.reshape(1, HEADS),
        attn_gain.reshape(1, width), moe_gain.reshape(1, width),
    )


def combine_kernel(cap, res_ref, normed_ref, router_ref, routes_ref, slots_ref, ret_ref, out_ref):
    rows = res_ref.shape[0]
    slots = ret_ref.shape[0]
    eye = lax.broadcasted_iota(jnp.int32, (rows, rows), 0) == lax.broadcasted_iota(
        jnp.int32, (rows, rows), 1
    )

    def column(row):
        wide = jnp.where(eye, row.astype(F32), 0.0)
        return jnp.sum(wide, axis=1, keepdims=True).astype(jnp.int32)

    routes = column(routes_ref[...])
    place = column(routes_ref[...] * cap + slots_ref[...])
    logits = dot(normed_ref[...], router_ref[...])
    expert = lax.broadcasted_iota(jnp.int32, logits.shape, 1)
    picked = jnp.sum(jnp.where(expert == routes, logits, 0.0), axis=1, keepdims=True)
    gate = jax.nn.sigmoid(picked)
    spot = lax.broadcasted_iota(jnp.int32, (rows, slots), 1)
    one_hot = jnp.where(spot == place, 1.0, 0.0).astype(BF16)
    out_ref[...] = (res_ref[...] + gate * dot(one_hot, ret_ref[...])).astype(BF16)


def combine(residual, normed, router, routes, slot_ids, returned, cap):
    rows, width = residual.shape
    step = WTOK
    rows_block = pl.BlockSpec((step, width), lambda i: (i, 0))
    ids_block = pl.BlockSpec((1, step), lambda i: (0, i))
    return pl.pallas_call(
        functools.partial(combine_kernel, cap),
        grid=(rows // step,),
        out_shape=jax.ShapeDtypeStruct((rows, width), BF16),
        in_specs=[
            rows_block, rows_block, whole_block(router.shape), ids_block, ids_block,
            whole_block(returned.shape),
        ],
        out_specs=rows_block,
        compiler_params=pltpu.CompilerParams(vmem_limit_bytes=48 * MIB),
        name="combine",
    )(residual, normed, router, routes.reshape(1, rows), slot_ids.reshape(1, rows), returned)


MESH = pl.DeviceIdType.MESH


def gather_kernel(shards_total, *refs):
    wqkv_ref, wproj_ref, net_ref, qkv_out, proj_out, net_out = refs[:6]
    up_send, up_recv, down_send, down_recv, sib_send, sib_recv, local = refs[6:]
    me = lax.axis_index("fsdp")
    rank = lax.axis_index("expert")
    core = lax.rem(rank, 2)
    sibling = {"expert": rank + 1 - 2 * core}
    above, below = {"fsdp": me + 1}, {"fsdp": me - 1}
    has_above, has_below = me + 1 < shards_total, me >= 1
    rows = wqkv_ref.shape[0]
    half = rows // 2
    width = wproj_ref.shape[1]

    barrier = pltpu.get_barrier_semaphore()

    @pl.when(has_above)
    def _():
        pl.semaphore_signal(barrier, inc=1, device_id=above, device_id_type=MESH)

    @pl.when(has_below)
    def _():
        pl.semaphore_signal(barrier, inc=1, device_id=below, device_id_type=MESH)

    pl.semaphore_signal(barrier, inc=1, device_id=sibling, device_id_type=MESH)

    peers = 1 + has_above.astype(jnp.int32) + has_below.astype(jnp.int32)
    pl.semaphore_wait(barrier, peers)

    pieces = ["net"]
    for c in range(wqkv_ref.shape[1] // width):
        pieces.append((wqkv_ref, qkv_out, c * width))
    pieces.append((wproj_ref, proj_out, 0))

    def place(piece, shard, part):
        if piece == "net":
            return net_out.at[shard]
        _, out, col = piece
        start = pl.multiple_of(shard * rows + part * half, half)
        return out.at[pl.ds(start, half), pl.ds(col, width)]

    def own(piece):
        if piece == "net":
            return net_ref
        ref, _, col = piece
        return ref.at[pl.ds(pl.multiple_of(core * half, half), half), pl.ds(col, width)]

    def hop(piece, p, step, shard, upward):
        send, recv = (up_send, up_recv) if upward else (down_send, down_recv)
        target = place(piece, shard, core)
        return pltpu.make_async_remote_copy(
            src_ref=own(piece) if step == 0 else target,
            dst_ref=target,
            send_sem=send.at[step, p],
            recv_sem=recv.at[step, p],
            device_id=above if upward else below,
            device_id_type=MESH,
        )

    def aside(piece, p, slot, shard, part):
        block = place(piece, shard, part)
        return pltpu.make_async_remote_copy(
            src_ref=block,
            dst_ref=block,
            send_sem=sib_send.at[slot, p],
            recv_sem=sib_recv.at[slot, p],
            device_id=sibling,
            device_id_type=MESH,
        )

    locals_ = [
        pltpu.make_async_copy(
            wqkv_ref, qkv_out.at[pl.ds(pl.multiple_of(me * rows, rows), rows)], local.at[0]
        ),
        pltpu.make_async_copy(
            wproj_ref, proj_out.at[pl.ds(pl.multiple_of(me * rows, rows), rows)], local.at[1]
        ),
        pltpu.make_async_copy(net_ref, net_out.at[me], local.at[2]),
    ]
    steps = shards_total - 1
    for step in range(steps + 1):
        for p, piece in enumerate(pieces):
            for upward in (True, False):
                sign = -1 if upward else 1
                shard = me + sign * step
                held = (shard >= 0) if upward else (shard < shards_total)
                further = has_above if upward else has_below
                if step > 0:
                    slot = (step - 1) * 2 + (0 if upward else 1)

                    @pl.when(held)
                    def _():
                        hop(piece, p, step - 1, shard, upward).wait_recv()
                        if piece != "net":
                            aside(piece, p, slot, shard, core).start()

                if step < steps:

                    @pl.when(held & further)
                    def _():
                        hop(piece, p, step, shard, upward).start()

        if step == 0:
            for copy in locals_:
                copy.start()
    for step in range(steps + 1):
        for p, piece in enumerate(pieces):
            for upward in (True, False):
                sign = -1 if upward else 1
                shard = me + sign * step
                held = (shard >= 0) if upward else (shard < shards_total)
                further = has_above if upward else has_below
                if step > 0 and piece != "net":
                    slot = (step - 1) * 2 + (0 if upward else 1)

                    @pl.when(held)
                    def _():
                        aside(piece, p, slot, shard, core).wait_send()
                        aside(piece, p, slot, shard, 1 - core).wait_recv()

                if step < steps:

                    @pl.when(held & further)
                    def _():
                        hop(piece, p, step, shard, upward).wait_send()

    for copy in locals_:
        copy.wait()


def gather_weights(qkv_weight, proj_weight, net):
    total = lax.axis_size("fsdp")
    rows, width = proj_weight.shape
    pieces = qkv_weight.shape[1] // width + 2
    anywhere = pl.BlockSpec(memory_space=pl.ANY)
    dma = pltpu.SemaphoreType.DMA
    return pl.pallas_call(
        functools.partial(gather_kernel, total),
        out_shape=(
            jax.ShapeDtypeStruct((total * rows, qkv_weight.shape[1]), BF16),
            jax.ShapeDtypeStruct((total * rows, width), BF16),
            jax.ShapeDtypeStruct((total,) + net.shape, F32),
        ),
        in_specs=[anywhere] * 3,
        out_specs=(anywhere,) * 3,
        scratch_shapes=[dma((total - 1, pieces)) for _ in range(4)]
        + [dma((2 * (total - 1), pieces)) for _ in range(2)]
        + [dma((3,))],
        compiler_params=pltpu.CompilerParams(collective_id=0, has_side_effects=True),
        name="gather_weights",
    )(qkv_weight, proj_weight, net)


def expert_kernel(chips, held, capp, *refs):
    normed_ref, routes_ref, slots_ref, win_any, wout_any, ret_ref = refs[:6]
    packed, arrived, answers, win, wout = refs[6:11]
    load, out_send, out_recv, back_send, back_recv, keep = refs[11:]
    rank = lax.axis_index("expert")
    chip, core = rank // 2, lax.rem(rank, 2)

    def rank_of(offset, which):
        return lax.rem(chip + offset, chips) * 2 + which

    barrier = pltpu.get_barrier_semaphore()
    for offset in range(1, 2 * chips):
        other = lax.rem(rank + offset, 2 * chips)
        pl.semaphore_signal(barrier, inc=1, device_id={"expert": other}, device_id_type=MESH)

    loads = []
    for e in range(held):
        loads.append(
            (
                pltpu.make_async_copy(win_any.at[e], win.at[e], load.at[2 * e]),
                pltpu.make_async_copy(wout_any.at[e], wout.at[e], load.at[2 * e + 1]),
            )
        )
        loads[e][0].start()
        loads[e][1].start()

    tokens = normed_ref.shape[0]
    spot = lax.broadcasted_iota(jnp.int32, (capp, tokens), 0)

    def pack(expert):
        hit = (spot == slots_ref[...]) & (routes_ref[...] == expert)
        return dot(jnp.where(hit, 1.0, 0.0).astype(BF16), normed_ref[...]).astype(BF16)

    def spread(k, which, e):
        far = (chips - k) % chips
        target = rank_of(k, which)
        return pltpu.make_async_remote_copy(
            src_ref=packed.at[target * held + e],
            dst_ref=arrived.at[far, e, core],
            send_sem=out_send.at[k, which, e],
            recv_sem=out_recv.at[far, core, e],
            device_id={"expert": target},
            device_id_type=MESH,
        )

    def spread_arrival(k, which, e):
        target = rank_of(k, which)
        return pltpu.make_async_remote_copy(
            src_ref=packed.at[target * held + e],
            dst_ref=arrived.at[k, e, which],
            send_sem=out_send.at[k, which, e],
            recv_sem=out_recv.at[k, which, e],
            device_id={"expert": target},
            device_id_type=MESH,
        )

    def back(k, which, e):
        target = rank_of(k, which)
        return pltpu.make_async_remote_copy(
            src_ref=answers.at[k, e, which],
            dst_ref=ret_ref.at[rank * held + e],
            send_sem=back_send.at[k, which, e],
            recv_sem=back_recv.at[(chips - k) % chips, core, e],
            device_id={"expert": target},
            device_id_type=MESH,
        )

    def back_arrival(k, which, e):
        target = rank_of(k, which)
        return pltpu.make_async_remote_copy(
            src_ref=answers.at[k, e, which],
            dst_ref=ret_ref.at[target * held + e],
            send_sem=back_send.at[k, which, e],
            recv_sem=back_recv.at[k, which, e],
            device_id={"expert": target},
            device_id_type=MESH,
        )

    def partners(k):
        return (0, 1) if k else (1 - core,)

    first = True
    for k in list(range(1, chips)) + [0]:
        for e in range(held):
            for which in partners(k):
                expert = rank_of(k, which) * held + e
                packed[expert] = pack(expert)
                if first:
                    pl.semaphore_wait(barrier, 2 * chips - 1)
                    first = False
                spread(k, which, e).start()
    for e in range(held):
        arrived[0, e, core] = pack(rank * held + e)

    ff = win.shape[2]
    chunk = 512
    for k in range(chips):
        for e in range(held):
            if k == 0:
                loads[e][0].wait()
                loads[e][1].wait()
            for which in partners(k):
                spread_arrival(k, which, e).wait_recv()
            x = arrived[k, e].reshape(2 * capp, arrived.shape[-1])
            total = None
            for f in range(0, ff, chunk):
                inner = dot(x, win[e, :, f : f + chunk])
                inner = (0.5 * inner * (1.0 + lax.erf(inner * math.sqrt(0.5)))).astype(BF16)
                part = dot(inner, wout[e, f : f + chunk, :])
                total = part if total is None else total + part
            answers[k, e] = total.astype(BF16).reshape(2, capp, arrived.shape[-1])
            for which in partners(k):
                back(k, which, e).start()
            if k == 0:
                pltpu.make_async_copy(
                    answers.at[0, e, core], ret_ref.at[rank * held + e], keep.at[e]
                ).start()
    for k in range(chips):
        for e in range(held):
            for which in partners(k):
                spread(k, which, e).wait_send()
                back(k, which, e).wait_send()
                back_arrival(k, which, e).wait_recv()
    for e in range(held):
        pltpu.make_async_copy(
            answers.at[0, e, core], ret_ref.at[rank * held + e], keep.at[e]
        ).wait()


def run_experts(normed, routes, slot_ids, expert_in, expert_out, experts, capp):
    rows, width = normed.shape
    held, _, ff = expert_in.shape
    chips = lax.axis_size("expert") // 2
    anywhere = pl.BlockSpec(memory_space=pl.ANY)
    near = pl.BlockSpec(memory_space=pltpu.VMEM)
    dma = pltpu.SemaphoreType.DMA
    return pl.pallas_call(
        functools.partial(expert_kernel, chips, held, capp),
        out_shape=jax.ShapeDtypeStruct((experts, capp, width), BF16),
        in_specs=[near, near, near, anywhere, anywhere],
        out_specs=anywhere,
        scratch_shapes=[
            pltpu.VMEM((experts, capp, width), BF16),
            pltpu.VMEM((chips, held, 2, capp, width), BF16),
            pltpu.VMEM((chips, held, 2, capp, width), BF16),
            pltpu.VMEM((held, width, ff), BF16),
            pltpu.VMEM((held, ff, width), BF16),
            dma((2 * held,)),
            dma((chips, 2, held)),
            dma((chips, 2, held)),
            dma((chips, 2, held)),
            dma((chips, 2, held)),
            dma((held,)),
        ],
        compiler_params=pltpu.CompilerParams(
            collective_id=1, has_side_effects=True, vmem_limit_bytes=48 * MIB
        ),
        name="experts",
    )(normed, routes.reshape(1, rows), slot_ids.reshape(1, rows), expert_in, expert_out)


def shards(
    tokens, routes, slot_ids, qkv_weight, proj_weight, logit_scale, first_weight, first_offset,
    second_weight, attn_gain, router, moe_gain, expert_in, expert_out,
):
    rows, width = tokens.shape
    units = first_weight.shape[1]
    net = jnp.concatenate(
        [second_weight.T, first_weight, first_offset[None], jnp.zeros((5, units), F32)], axis=0
    )
    wqkv, wproj, net = gather_weights(qkv_weight, proj_weight, net)
    residual, normed = attention(tokens, wqkv, wproj, net, logit_scale, attn_gain, moe_gain)
    experts = router.shape[1]
    cap = rows * 5 // (4 * experts)
    capp = (cap + 15) // 16 * 16
    returned = run_experts(normed, routes, slot_ids, expert_in, expert_out, experts, capp)
    returned = returned.reshape(experts * capp, width)
    return combine(residual, normed, router, routes, slot_ids, returned, capp)


def solution(mesh):
    rows = P(("groups", "expert", "fsdp"))
    return jax.shard_map(
        shards,
        mesh=mesh,
        in_specs=(
            P(("groups", "expert", "fsdp"), None), rows, rows, P("fsdp", None), P("fsdp", None),
            P(), P(None, "fsdp"), P("fsdp"), P("fsdp", None), P(), P(), P(),
            P("expert", None, None), P("expert", None, None),
        ),
        out_specs=P(("groups", "expert", "fsdp"), None),
        check_vma=False,
    )
```

```python
import functools
import math

import jax
import jax.numpy as jnp
import numpy as np
from jax import lax
from jax.experimental import pallas as pl
from jax.experimental.pallas import tpu as pltpu
from jax.sharding import PartitionSpec as P

HEADS = 16
WIN = 16
WTOK = WIN * WIN
LOG2E = math.log2(math.e)
NORM_EPS = 1e-05
UNIT_EPS = 1e-06
HIGHEST = lax.Precision.HIGHEST
MIB = 1024 * 1024
F32 = jnp.float32
BF16 = jnp.bfloat16


def table_coords():
    offsets = (WIN - 1 - np.arange(32)).astype(np.float32)
    stretched = offsets / np.float32(WIN - 1) * np.float32(8.0)
    logged = np.sign(stretched) * np.log2(np.abs(stretched) + np.float32(1.0)) / np.float32(3.0)
    logged = logged.astype(np.float32)
    out = np.zeros((1024, 8), np.float32)
    out[:, 0] = np.repeat(logged, 32)
    out[:, 1] = np.tile(logged, 32)
    return out


def layer_norm(values, gain):
    centre = values - jnp.mean(values, axis=-1, keepdims=True)
    spread = jnp.mean(centre * centre, axis=-1, keepdims=True)
    return centre * lax.rsqrt(spread + NORM_EPS) * gain


def dot(a, b):
    return jnp.dot(a, b, preferred_element_type=F32)


def dot_nt(a, b, precision=None):
    return lax.dot_general(
        a, b, (((1,), (1,)), ((), ())), precision=precision, preferred_element_type=F32
    )


def build_bias(net_ref, coords_ref, strips, bias):
    shard_count = net_ref.shape[0]
    c0 = coords_ref[:, 0:1]
    c1 = coords_ref[:, 1:2]
    table = None
    for z in range(shard_count):
        hidden = c0 * net_ref[z, 16:17, :] + c1 * net_ref[z, 17:18, :] + net_ref[z, 18:19, :]
        hidden = jnp.maximum(hidden, 0.0)
        part = dot_nt(net_ref[z, 0:16, :], hidden, HIGHEST)
        table = part if table is None else table + part
    table = (16.0 * LOG2E) * jax.nn.sigmoid(table)
    stacked = jnp.concatenate([table[:, g * 256 : (g + 1) * 256] for g in range(4)], axis=0)
    high = stacked.astype(BF16)
    rest = stacked - high.astype(F32)
    mid = rest.astype(BF16)
    low = (rest - mid.astype(F32)).astype(BF16)
    pieces = jnp.concatenate([high, mid, low], axis=0)
    k = lax.broadcasted_iota(jnp.int32, (256, 128), 0)
    c = lax.broadcasted_iota(jnp.int32, (256, 128), 1)
    same_row = (k // 32) == (c // 16)
    shift = (k % 32) - (c % 16)
    for xi in range(16):
        sel = jnp.where(same_row & (shift == 15 - xi), 1.0, 0.0).astype(BF16)
        picked = dot(pieces, sel)
        strips[xi] = picked[0:64] + picked[64:128] + picked[128:192]
    for h in range(HEADS):
        strip = jnp.concatenate([strips[:, g * 16 + h, :] for g in range(4)], axis=1)
        for yi in range(16):
            start = (15 - yi) * 16
            bias[h, yi * 16 : (yi + 1) * 16, :] = strip[:, start : start + 256]


def attention_kernel(
    tok_ref, wqkv_ref, wproj_ref, net_ref, coords_ref, ls_ref, ag_ref, mg_ref,
    res_ref, normed_ref, strips, bias, ones_ref, ctx_ref,
):
    @pl.when(pl.program_id(0) == 0)
    def _():
        build_bias(net_ref, coords_ref, strips, bias)
        r = lax.broadcasted_iota(jnp.int32, ones_ref.shape, 0)
        c = lax.broadcasted_iota(jnp.int32, ones_ref.shape, 1)
        ones_ref[...] = jnp.where((r // 32) == (c // 32), 1.0, 0.0).astype(BF16)

    width = tok_ref.shape[1]
    tok = tok_ref[...]
    scales = jnp.exp(jnp.minimum(ls_ref[...], math.log(100.0))) * LOG2E
    lane = lax.broadcasted_iota(jnp.int32, (WTOK, 128), 1) // 32

    def unit(col):
        x = dot(tok, wqkv_ref[:, col : col + 256])
        sq = x * x
        high = sq.astype(BF16)
        low = (sq - high.astype(F32)).astype(BF16)
        ones = ones_ref[...]
        total = dot(high, ones) + dot(low, ones)
        return (x * lax.rsqrt(total + UNIT_EPS)).astype(BF16)

    for pair in range(width // 256):
        base = pair * 256
        uq2 = unit(base)
        uk2 = unit(width + base)
        v2 = dot(tok, wqkv_ref[:, 2 * width + base : 2 * width + base + 256]).astype(BF16)
        for half in range(2):
            uq = uq2[:, half * 128 : (half + 1) * 128]
            uk = uk2[:, half * 128 : (half + 1) * 128]
            v = v2[:, half * 128 : (half + 1) * 128]
            ctx = None
            for j in range(4):
                h = pair * 8 + half * 4 + j
                q = jnp.where(lane == j, uq, jnp.zeros_like(uq))
                s = dot_nt(q, uk) * scales[:, h : h + 1] + bias[h]
                e = jnp.exp2(s - jnp.max(s, axis=-1, keepdims=True))
                w = (e * (1.0 / jnp.sum(e, axis=-1, keepdims=True))).astype(BF16)
                o = dot(w, v)
                ctx = o if ctx is None else jnp.where(lane == j, o, ctx)
            ctx_ref[:, base + half * 128 : base + (half + 1) * 128] = ctx.astype(BF16)

    attended = dot(ctx_ref[...], wproj_ref[...])
    residual = tok.astype(F32) + layer_norm(attended, ag_ref[...])
    res_ref[...] = residual
    normed_ref[...] = layer_norm(residual, mg_ref[...]).astype(BF16)


def whole_block(shape):
    return pl.BlockSpec(shape, lambda i: (0,) * len(shape))


def attention(tokens, wqkv, wproj, net, logit_scale, attn_gain, moe_gain):
    rows, width = tokens.shape
    coords = jnp.asarray(table_coords())
    rows_block = pl.BlockSpec((WTOK, width), lambda i: (i, 0))
    return pl.pallas_call(
        attention_kernel,
        grid=(rows // WTOK,),
        out_shape=(
            jax.ShapeDtypeStruct((rows, width), F32),
            jax.ShapeDtypeStruct((rows, width), BF16),
        ),
        in_specs=[
            rows_block,
            whole_block(wqkv.shape),
            whole_block(wproj.shape),
            whole_block(net.shape),
            whole_block(coords.shape),
            whole_block((1, HEADS)),
            whole_block((1, width)),
            whole_block((1, width)),
        ],
        out_specs=(rows_block, rows_block),
        scratch_shapes=[
            pltpu.VMEM((16, 64, 128), F32),
            pltpu.VMEM((HEADS, WTOK, WTOK), F32),
            pltpu.VMEM((256, 256), BF16),
            pltpu.VMEM((WTOK, width), BF16),
        ],
        compiler_params=pltpu.CompilerParams(vmem_limit_bytes=60 * MIB),
        name="attention",
    )(
        tokens, wqkv, wproj, net, coords, logit_scale.reshape(1, HEADS),
        attn_gain.reshape(1, width), moe_gain.reshape(1, width),
    )


def combine_kernel(cap, res_ref, normed_ref, router_ref, routes_ref, slots_ref, ret_ref, out_ref):
    rows = res_ref.shape[0]
    slots = ret_ref.shape[0]
    eye = lax.broadcasted_iota(jnp.int32, (rows, rows), 0) == lax.broadcasted_iota(
        jnp.int32, (rows, rows), 1
    )

    def column(row):
        wide = jnp.where(eye, row.astype(F32), 0.0)
        return jnp.sum(wide, axis=1, keepdims=True).astype(jnp.int32)

    routes = column(routes_ref[...])
    place = column(routes_ref[...] * cap + slots_ref[...])
    logits = dot(normed_ref[...], router_ref[...])
    expert = lax.broadcasted_iota(jnp.int32, logits.shape, 1)
    picked = jnp.sum(jnp.where(expert == routes, logits, 0.0), axis=1, keepdims=True)
    gate = jax.nn.sigmoid(picked)
    spot = lax.broadcasted_iota(jnp.int32, (rows, slots), 1)
    one_hot = jnp.where(spot == place, 1.0, 0.0).astype(BF16)
    out_ref[...] = (res_ref[...] + gate * dot(one_hot, ret_ref[...])).astype(BF16)


def combine(residual, normed, router, routes, slot_ids, returned, cap):
    rows, width = residual.shape
    step = WTOK
    rows_block = pl.BlockSpec((step, width), lambda i: (i, 0))
    ids_block = pl.BlockSpec((1, step), lambda i: (0, i))
    return pl.pallas_call(
        functools.partial(combine_kernel, cap),
        grid=(rows // step,),
        out_shape=jax.ShapeDtypeStruct((rows, width), BF16),
        in_specs=[
            rows_block, rows_block, whole_block(router.shape), ids_block, ids_block,
            whole_block(returned.shape),
        ],
        out_specs=rows_block,
        compiler_params=pltpu.CompilerParams(vmem_limit_bytes=60 * MIB),
        name="combine",
    )(residual, normed, router, routes.reshape(1, rows), slot_ids.reshape(1, rows), returned)


MESH = pl.DeviceIdType.MESH


def gather_kernel(shards_total, *refs):
    wqkv_ref, wproj_ref, net_ref, qkv_out, proj_out, net_out = refs[:6]
    up_send, up_recv, down_send, down_recv = refs[6:10]
    sib_send, sib_recv, far_send, far_recv, on_send, on_recv, local = refs[10:]
    me = lax.axis_index("fsdp")
    rank = lax.axis_index("expert")
    core = lax.rem(rank, 2)
    side = lax.rem(rank // 2, 2)
    mine, theirs = side * 2 + core, (1 - side) * 2 + core
    sibling = {"expert": rank + 1 - 2 * core}
    across = {"expert": rank + 2 - 4 * side}
    above, below = {"fsdp": me + 1}, {"fsdp": me - 1}
    has_above, has_below = me + 1 < shards_total, me >= 1
    rows = wqkv_ref.shape[0]
    quarter = rows // 4

    barrier = pltpu.get_barrier_semaphore()

    @pl.when(has_above)
    def _():
        pl.semaphore_signal(barrier, inc=1, device_id=above, device_id_type=MESH)

    @pl.when(has_below)
    def _():
        pl.semaphore_signal(barrier, inc=1, device_id=below, device_id_type=MESH)

    pl.semaphore_signal(barrier, inc=1, device_id=sibling, device_id_type=MESH)
    pl.semaphore_signal(barrier, inc=1, device_id=across, device_id_type=MESH)

    peers = 2 + has_above.astype(jnp.int32) + has_below.astype(jnp.int32)
    pl.semaphore_wait(barrier, peers)

    pieces = ["net", (wqkv_ref, qkv_out), (wproj_ref, proj_out)]

    def place(piece, shard, part):
        if piece == "net":
            return net_out.at[shard]
        start = pl.multiple_of(shard * rows + part * quarter, quarter)
        return piece[1].at[pl.ds(start, quarter)]

    def own(piece):
        if piece == "net":
            return net_ref
        return piece[0].at[pl.ds(pl.multiple_of(mine * quarter, quarter), quarter)]

    def hop(piece, p, step, shard, upward):
        send, recv = (up_send, up_recv) if upward else (down_send, down_recv)
        target = place(piece, shard, mine)
        return pltpu.make_async_remote_copy(
            src_ref=own(piece) if step == 0 else target,
            dst_ref=target,
            send_sem=send.at[step, p],
            recv_sem=recv.at[step, p],
            device_id=above if upward else below,
            device_id_type=MESH,
        )

    def push(piece, p, slot, shard, part, sems, device):
        block = place(piece, shard, part)
        return pltpu.make_async_remote_copy(
            src_ref=block,
            dst_ref=block,
            send_sem=sems[0].at[slot, p],
            recv_sem=sems[1].at[slot, p],
            device_id=device,
            device_id_type=MESH,
        )

    near_sems, far_sems, on_sems = (sib_send, sib_recv), (far_send, far_recv), (on_send, on_recv)

    def hand_on(step, p, piece):
        for upward in (True, False):
            shard = me - step if upward else me + step
            held = (shard >= 0) if upward else (shard < shards_total)
            slot = (step - 1) * 2 + (0 if upward else 1)

            @pl.when(held)
            def _():
                push(piece, p, slot, shard, theirs, far_sems, across).wait_recv()
                push(piece, p, slot, shard, theirs, on_sems, sibling).start()

    locals_ = [
        pltpu.make_async_copy(
            wqkv_ref, qkv_out.at[pl.ds(pl.multiple_of(me * rows, rows), rows)], local.at[0]
        ),
        pltpu.make_async_copy(
            wproj_ref, proj_out.at[pl.ds(pl.multiple_of(me * rows, rows), rows)], local.at[1]
        ),
        pltpu.make_async_copy(net_ref, net_out.at[me], local.at[2]),
    ]
    steps = shards_total - 1
    for step in range(steps + 1):
        for p, piece in enumerate(pieces):
            for upward in (True, False):
                sign = -1 if upward else 1
                shard = me + sign * step
                held = (shard >= 0) if upward else (shard < shards_total)
                further = has_above if upward else has_below
                if step > 0:
                    slot = (step - 1) * 2 + (0 if upward else 1)

                    @pl.when(held)
                    def _():
                        hop(piece, p, step - 1, shard, upward).wait_recv()
                        if piece != "net":
                            push(piece, p, slot, shard, mine, far_sems, across).start()
                            push(piece, p, slot, shard, mine, near_sems, sibling).start()

                if step < steps:

                    @pl.when(held & further)
                    def _():
                        hop(piece, p, step, shard, upward).start()

            if step > 1 and piece != "net":
                hand_on(step - 1, p, piece)

        if step == 0:
            for copy in locals_:
                copy.start()
    for p, piece in enumerate(pieces):
        if piece != "net":
            hand_on(steps, p, piece)
    for step in range(steps + 1):
        for p, piece in enumerate(pieces):
            for upward in (True, False):
                sign = -1 if upward else 1
                shard = me + sign * step
                held = (shard >= 0) if upward else (shard < shards_total)
                further = has_above if upward else has_below
                if step > 0 and piece != "net":
                    slot = (step - 1) * 2 + (0 if upward else 1)

                    @pl.when(held)
                    def _():
                        beside = side * 2 + 1 - core
                        push(piece, p, slot, shard, mine, far_sems, across).wait_send()
                        push(piece, p, slot, shard, mine, near_sems, sibling).wait_send()
                        push(piece, p, slot, shard, theirs, on_sems, sibling).wait_send()
                        push(piece, p, slot, shard, beside, near_sems, sibling).wait_recv()
                        crossed = (1 - side) * 2 + 1 - core
                        push(piece, p, slot, shard, crossed, on_sems, sibling).wait_recv()

                if step < steps:

                    @pl.when(held & further)
                    def _():
                        hop(piece, p, step, shard, upward).wait_send()

    for copy in locals_:
        copy.wait()


def gather_weights(qkv_weight, proj_weight, net):
    total = lax.axis_size("fsdp")
    rows, width = proj_weight.shape
    pieces = 3
    anywhere = pl.BlockSpec(memory_space=pl.ANY)
    dma = pltpu.SemaphoreType.DMA
    return pl.pallas_call(
        functools.partial(gather_kernel, total),
        out_shape=(
            jax.ShapeDtypeStruct((total * rows, qkv_weight.shape[1]), BF16),
            jax.ShapeDtypeStruct((total * rows, width), BF16),
            jax.ShapeDtypeStruct((total,) + net.shape, F32),
        ),
        in_specs=[anywhere] * 3,
        out_specs=(anywhere,) * 3,
        scratch_shapes=[dma((total - 1, pieces)) for _ in range(4)]
        + [dma((2 * (total - 1), pieces)) for _ in range(6)]
        + [dma((3,))],
        compiler_params=pltpu.CompilerParams(collective_id=0, has_side_effects=True),
        name="gather_weights",
    )(qkv_weight, proj_weight, net)


def expert_kernel(chips, held, capp, *refs):
    normed_ref, routes_ref, slots_ref, win_any, wout_any, ret_ref = refs[:6]
    packed, arrived, answers, win, wout = refs[6:11]
    load, out_send, out_recv, back_send, back_recv, keep = refs[11:]
    rank = lax.axis_index("expert")
    chip, core = rank // 2, lax.rem(rank, 2)

    def rank_of(offset, which):
        return lax.rem(chip + offset, chips) * 2 + which

    barrier = pltpu.get_barrier_semaphore()
    for offset in range(1, 2 * chips):
        other = lax.rem(rank + offset, 2 * chips)
        pl.semaphore_signal(barrier, inc=1, device_id={"expert": other}, device_id_type=MESH)

    loads = []
    for e in range(held):
        loads.append(
            (
                pltpu.make_async_copy(win_any.at[e], win.at[e], load.at[2 * e]),
                pltpu.make_async_copy(wout_any.at[e], wout.at[e], load.at[2 * e + 1]),
            )
        )
        loads[e][0].start()
        loads[e][1].start()

    tokens = normed_ref.shape[0]
    spot = lax.broadcasted_iota(jnp.int32, (capp, tokens), 0)

    def pack(expert):
        hit = (spot == slots_ref[...]) & (routes_ref[...] == expert)
        return dot(jnp.where(hit, 1.0, 0.0).astype(BF16), normed_ref[...]).astype(BF16)

    def spread(k, which, e):
        far = (chips - k) % chips
        target = rank_of(k, which)
        return pltpu.make_async_remote_copy(
            src_ref=packed.at[target * held + e],
            dst_ref=arrived.at[far, e, core],
            send_sem=out_send.at[k, which, e],
            recv_sem=out_recv.at[far, core, e],
            device_id={"expert": target},
            device_id_type=MESH,
        )

    def spread_arrival(k, which, e):
        target = rank_of(k, which)
        return pltpu.make_async_remote_copy(
            src_ref=packed.at[target * held + e],
            dst_ref=arrived.at[k, e, which],
            send_sem=out_send.at[k, which, e],
            recv_sem=out_recv.at[k, which, e],
            device_id={"expert": target},
            device_id_type=MESH,
        )

    def back(k, which, e):
        target = rank_of(k, which)
        return pltpu.make_async_remote_copy(
            src_ref=answers.at[k, e, which],
            dst_ref=ret_ref.at[rank * held + e],
            send_sem=back_send.at[k, which, e],
            recv_sem=back_recv.at[(chips - k) % chips, core, e],
            device_id={"expert": target},
            device_id_type=MESH,
        )

    def back_arrival(k, which, e):
        target = rank_of(k, which)
        return pltpu.make_async_remote_copy(
            src_ref=answers.at[k, e, which],
            dst_ref=ret_ref.at[target * held + e],
            send_sem=back_send.at[k, which, e],
            recv_sem=back_recv.at[k, which, e],
            device_id={"expert": target},
            device_id_type=MESH,
        )

    def partners(k):
        return (0, 1) if k else (1 - core,)

    first = True
    for k in list(range(1, chips)) + [0]:
        for e in range(held):
            for which in partners(k):
                expert = rank_of(k, which) * held + e
                packed[expert] = pack(expert)
                if first:
                    pl.semaphore_wait(barrier, 2 * chips - 1)
                    first = False
                spread(k, which, e).start()
    for e in range(held):
        arrived[0, e, core] = pack(rank * held + e)

    ff = win.shape[2]
    chunk = 512
    for k in range(chips):
        for e in range(held):
            if k == 0:
                loads[e][0].wait()
                loads[e][1].wait()
            for which in partners(k):
                spread_arrival(k, which, e).wait_recv()
            x = arrived[k, e].reshape(2 * capp, arrived.shape[-1])
            total = None
            for f in range(0, ff, chunk):
                inner = dot(x, win[e, :, f : f + chunk])
                inner = (0.5 * inner * (1.0 + lax.erf(inner * math.sqrt(0.5)))).astype(BF16)
                part = dot(inner, wout[e, f : f + chunk, :])
                total = part if total is None else total + part
            answers[k, e] = total.astype(BF16).reshape(2, capp, arrived.shape[-1])
            for which in partners(k):
                back(k, which, e).start()
            if k == 0:
                pltpu.make_async_copy(
                    answers.at[0, e, core], ret_ref.at[rank * held + e], keep.at[e]
                ).start()
    for k in range(chips):
        for e in range(held):
            for which in partners(k):
                spread(k, which, e).wait_send()
                back(k, which, e).wait_send()
                back_arrival(k, which, e).wait_recv()
    for e in range(held):
        pltpu.make_async_copy(
            answers.at[0, e, core], ret_ref.at[rank * held + e], keep.at[e]
        ).wait()


def run_experts(normed, routes, slot_ids, expert_in, expert_out, experts, capp):
    rows, width = normed.shape
    held, _, ff = expert_in.shape
    chips = lax.axis_size("expert") // 2
    anywhere = pl.BlockSpec(memory_space=pl.ANY)
    near = pl.BlockSpec(memory_space=pltpu.VMEM)
    dma = pltpu.SemaphoreType.DMA
    return pl.pallas_call(
        functools.partial(expert_kernel, chips, held, capp),
        out_shape=jax.ShapeDtypeStruct((experts, capp, width), BF16),
        in_specs=[near, near, near, anywhere, anywhere],
        out_specs=anywhere,
        scratch_shapes=[
            pltpu.VMEM((experts, capp, width), BF16),
            pltpu.VMEM((chips, held, 2, capp, width), BF16),
            pltpu.VMEM((chips, held, 2, capp, width), BF16),
            pltpu.VMEM((held, width, ff), BF16),
            pltpu.VMEM((held, ff, width), BF16),
            dma((2 * held,)),
            dma((chips, 2, held)),
            dma((chips, 2, held)),
            dma((chips, 2, held)),
            dma((chips, 2, held)),
            dma((held,)),
        ],
        compiler_params=pltpu.CompilerParams(
            collective_id=1, has_side_effects=True, vmem_limit_bytes=60 * MIB
        ),
        name="experts",
    )(normed, routes.reshape(1, rows), slot_ids.reshape(1, rows), expert_in, expert_out)


def shards(
    tokens, routes, slot_ids, qkv_weight, proj_weight, logit_scale, first_weight, first_offset,
    second_weight, attn_gain, router, moe_gain, expert_in, expert_out,
):
    rows, width = tokens.shape
    units = first_weight.shape[1]
    net = jnp.concatenate(
        [second_weight.T, first_weight, first_offset[None], jnp.zeros((5, units), F32)], axis=0
    )
    wqkv, wproj, net = gather_weights(qkv_weight, proj_weight, net)
    residual, normed = attention(tokens, wqkv, wproj, net, logit_scale, attn_gain, moe_gain)
    experts = router.shape[1]
    cap = rows * 5 // (4 * experts)
    capp = (cap + 15) // 16 * 16
    returned = run_experts(normed, routes, slot_ids, expert_in, expert_out, experts, capp)
    returned = returned.reshape(experts * capp, width)
    return combine(residual, normed, router, routes, slot_ids, returned, capp)


def solution(mesh):
    rows = P(("groups", "expert", "fsdp"))
    return jax.shard_map(
        shards,
        mesh=mesh,
        in_specs=(
            P(("groups", "expert", "fsdp"), None), rows, rows, P("fsdp", None), P("fsdp", None),
            P(), P(None, "fsdp"), P("fsdp"), P("fsdp", None), P(), P(), P(),
            P("expert", None, None), P("expert", None, None),
        ),
        out_specs=P(("groups", "expert", "fsdp"), None),
        check_vma=False,
    )
```

```python
import functools
import math

import jax
import jax.numpy as jnp
import numpy as np
from jax import lax
from jax.experimental import pallas as pl
from jax.experimental.pallas import tpu as pltpu
from jax.sharding import PartitionSpec as P

HEADS = 16
WIN = 16
WTOK = WIN * WIN
LOG2E = math.log2(math.e)
NORM_EPS = 1e-05
UNIT_EPS = 1e-06
HIGHEST = lax.Precision.HIGHEST
MIB = 1024 * 1024
F32 = jnp.float32
BF16 = jnp.bfloat16


def table_coords():
    offsets = (WIN - 1 - np.arange(32)).astype(np.float32)
    stretched = offsets / np.float32(WIN - 1) * np.float32(8.0)
    logged = np.sign(stretched) * np.log2(np.abs(stretched) + np.float32(1.0)) / np.float32(3.0)
    logged = logged.astype(np.float32)
    out = np.zeros((1024, 8), np.float32)
    out[:, 0] = np.repeat(logged, 32)
    out[:, 1] = np.tile(logged, 32)
    return out


def layer_norm(values, gain):
    centre = values - jnp.mean(values, axis=-1, keepdims=True)
    spread = jnp.mean(centre * centre, axis=-1, keepdims=True)
    return centre * lax.rsqrt(spread + NORM_EPS) * gain


def dot(a, b):
    return jnp.dot(a, b, preferred_element_type=F32)


def dot_nt(a, b, precision=None):
    return lax.dot_general(
        a, b, (((1,), (1,)), ((), ())), precision=precision, preferred_element_type=F32
    )


def build_bias(net_ref, coords_ref, strips, bias):
    shard_count = net_ref.shape[0]
    c0 = coords_ref[:, 0:1]
    c1 = coords_ref[:, 1:2]
    table = None
    for z in range(shard_count):
        hidden = c0 * net_ref[z, 16:17, :] + c1 * net_ref[z, 17:18, :] + net_ref[z, 18:19, :]
        hidden = jnp.maximum(hidden, 0.0)
        part = dot_nt(net_ref[z, 0:16, :], hidden, HIGHEST)
        table = part if table is None else table + part
    table = (16.0 * LOG2E) * jax.nn.sigmoid(table)
    stacked = jnp.concatenate([table[:, g * 256 : (g + 1) * 256] for g in range(4)], axis=0)
    high = stacked.astype(BF16)
    rest = stacked - high.astype(F32)
    mid = rest.astype(BF16)
    low = (rest - mid.astype(F32)).astype(BF16)
    pieces = jnp.concatenate([high, mid, low], axis=0)
    k = lax.broadcasted_iota(jnp.int32, (256, 128), 0)
    c = lax.broadcasted_iota(jnp.int32, (256, 128), 1)
    same_row = (k // 32) == (c // 16)
    shift = (k % 32) - (c % 16)
    for xi in range(16):
        sel = jnp.where(same_row & (shift == 15 - xi), 1.0, 0.0).astype(BF16)
        picked = dot(pieces, sel)
        strips[xi] = picked[0:64] + picked[64:128] + picked[128:192]
    for h in range(HEADS):
        strip = jnp.concatenate([strips[:, g * 16 + h, :] for g in range(4)], axis=1)
        for yi in range(16):
            start = (15 - yi) * 16
            bias[h, yi * 16 : (yi + 1) * 16, :] = strip[:, start : start + 256]


def attention_kernel(
    tok_ref, wqkv_ref, wproj_ref, net_ref, coords_ref, ls_ref, ag_ref, mg_ref,
    res_ref, normed_ref, strips, bias, ones_ref, ctx_ref,
):
    @pl.when(pl.program_id(0) == 0)
    def _():
        build_bias(net_ref, coords_ref, strips, bias)
        r = lax.broadcasted_iota(jnp.int32, ones_ref.shape, 0)
        c = lax.broadcasted_iota(jnp.int32, ones_ref.shape, 1)
        ones_ref[...] = jnp.where((r // 32) == (c // 32), 1.0, 0.0).astype(BF16)

    width = tok_ref.shape[1]
    tok = tok_ref[...]
    scales = jnp.exp(jnp.minimum(ls_ref[...], math.log(100.0))) * LOG2E
    lane = lax.broadcasted_iota(jnp.int32, (WTOK, 128), 1) // 32

    def unit(col):
        x = dot(tok, wqkv_ref[:, col : col + 256])
        sq = x * x
        high = sq.astype(BF16)
        low = (sq - high.astype(F32)).astype(BF16)
        ones = ones_ref[...]
        total = dot(high, ones) + dot(low, ones)
        return (x * lax.rsqrt(total + UNIT_EPS)).astype(BF16)

    for pair in range(width // 256):
        base = pair * 256
        uq2 = unit(base)
        uk2 = unit(width + base)
        v2 = dot(tok, wqkv_ref[:, 2 * width + base : 2 * width + base + 256]).astype(BF16)
        for half in range(2):
            uq = uq2[:, half * 128 : (half + 1) * 128]
            uk = uk2[:, half * 128 : (half + 1) * 128]
            v = v2[:, half * 128 : (half + 1) * 128]
            ctx = None
            for j in range(4):
                h = pair * 8 + half * 4 + j
                q = jnp.where(lane == j, uq, jnp.zeros_like(uq))
                s = dot_nt(q, uk) * scales[:, h : h + 1] + bias[h]
                e = jnp.exp2(s - jnp.max(s, axis=-1, keepdims=True))
                w = (e * (1.0 / jnp.sum(e, axis=-1, keepdims=True))).astype(BF16)
                o = dot(w, v)
                ctx = o if ctx is None else jnp.where(lane == j, o, ctx)
            ctx_ref[:, base + half * 128 : base + (half + 1) * 128] = ctx.astype(BF16)

    attended = dot(ctx_ref[...], wproj_ref[...])
    residual = tok.astype(F32) + layer_norm(attended, ag_ref[...])
    res_ref[...] = residual
    normed_ref[...] = layer_norm(residual, mg_ref[...]).astype(BF16)


def whole_block(shape):
    return pl.BlockSpec(shape, lambda i: (0,) * len(shape))


def attention(tokens, wqkv, wproj, net, logit_scale, attn_gain, moe_gain):
    rows, width = tokens.shape
    coords = jnp.asarray(table_coords())
    rows_block = pl.BlockSpec((WTOK, width), lambda i: (i, 0))
    return pl.pallas_call(
        attention_kernel,
        grid=(rows // WTOK,),
        out_shape=(
            jax.ShapeDtypeStruct((rows, width), F32),
            jax.ShapeDtypeStruct((rows, width), BF16),
        ),
        in_specs=[
            rows_block,
            whole_block(wqkv.shape),
            whole_block(wproj.shape),
            whole_block(net.shape),
            whole_block(coords.shape),
            whole_block((1, HEADS)),
            whole_block((1, width)),
            whole_block((1, width)),
        ],
        out_specs=(rows_block, rows_block),
        scratch_shapes=[
            pltpu.VMEM((16, 64, 128), F32),
            pltpu.VMEM((HEADS, WTOK, WTOK), F32),
            pltpu.VMEM((256, 256), BF16),
            pltpu.VMEM((WTOK, width), BF16),
        ],
        compiler_params=pltpu.CompilerParams(vmem_limit_bytes=60 * MIB),
        name="attention",
    )(
        tokens, wqkv, wproj, net, coords, logit_scale.reshape(1, HEADS),
        attn_gain.reshape(1, width), moe_gain.reshape(1, width),
    )


def combine_kernel(cap, res_ref, normed_ref, router_ref, routes_ref, slots_ref, ret_ref, out_ref):
    rows = res_ref.shape[0]
    slots = ret_ref.shape[0]
    eye = lax.broadcasted_iota(jnp.int32, (rows, rows), 0) == lax.broadcasted_iota(
        jnp.int32, (rows, rows), 1
    )

    def column(row):
        wide = jnp.where(eye, row.astype(F32), 0.0)
        return jnp.sum(wide, axis=1, keepdims=True).astype(jnp.int32)

    routes = column(routes_ref[...])
    place = column(routes_ref[...] * cap + slots_ref[...])
    logits = dot_nt(normed_ref[...], router_ref[...])
    expert = lax.broadcasted_iota(jnp.int32, logits.shape, 1)
    picked = jnp.sum(jnp.where(expert == routes, logits, 0.0), axis=1, keepdims=True)
    gate = jax.nn.sigmoid(picked)
    spot = lax.broadcasted_iota(jnp.int32, (rows, slots), 1)
    one_hot = jnp.where(spot == place, 1.0, 0.0).astype(BF16)
    out_ref[...] = (res_ref[...] + gate * dot(one_hot, ret_ref[...])).astype(BF16)


def combine(residual, normed, router, routes, slot_ids, returned, cap):
    rows, width = residual.shape
    step = WTOK
    rows_block = pl.BlockSpec((step, width), lambda i: (i, 0))
    ids_block = pl.BlockSpec((1, step), lambda i: (0, i))
    return pl.pallas_call(
        functools.partial(combine_kernel, cap),
        grid=(rows // step,),
        out_shape=jax.ShapeDtypeStruct((rows, width), BF16),
        in_specs=[
            rows_block, rows_block, whole_block(router.shape), ids_block, ids_block,
            whole_block(returned.shape),
        ],
        out_specs=rows_block,
        compiler_params=pltpu.CompilerParams(vmem_limit_bytes=48 * MIB),
        name="combine",
    )(residual, normed, router, routes.reshape(1, rows), slot_ids.reshape(1, rows), returned)


MESH = pl.DeviceIdType.MESH


def gather_kernel(shards_total, *refs):
    wqkv_ref, wproj_ref, net_ref, qkv_out, proj_out, net_out = refs[:6]
    up_send, up_recv, down_send, down_recv = refs[6:10]
    sib_send, sib_recv, far_send, far_recv, on_send, on_recv, local = refs[10:]
    me = lax.axis_index("fsdp")
    rank = lax.axis_index("expert")
    core = lax.rem(rank, 2)
    side = lax.rem(rank // 2, 2)
    mine, theirs = side * 2 + core, (1 - side) * 2 + core
    sibling = {"expert": rank + 1 - 2 * core}
    across = {"expert": rank + 2 - 4 * side}
    above, below = {"fsdp": me + 1}, {"fsdp": me - 1}
    has_above, has_below = me + 1 < shards_total, me >= 1
    rows = wqkv_ref.shape[0]
    quarter = rows // 4

    barrier = pltpu.get_barrier_semaphore()

    @pl.when(has_above)
    def _():
        pl.semaphore_signal(barrier, inc=1, device_id=above, device_id_type=MESH)

    @pl.when(has_below)
    def _():
        pl.semaphore_signal(barrier, inc=1, device_id=below, device_id_type=MESH)

    pl.semaphore_signal(barrier, inc=1, device_id=sibling, device_id_type=MESH)
    pl.semaphore_signal(barrier, inc=1, device_id=across, device_id_type=MESH)

    peers = 2 + has_above.astype(jnp.int32) + has_below.astype(jnp.int32)
    pl.semaphore_wait(barrier, peers)

    pieces = ["net", (wqkv_ref, qkv_out), (wproj_ref, proj_out)]

    def place(piece, shard, part):
        if piece == "net":
            return net_out.at[shard]
        start = pl.multiple_of(shard * rows + part * quarter, quarter)
        return piece[1].at[pl.ds(start, quarter)]

    def own(piece):
        if piece == "net":
            return net_ref
        return piece[0].at[pl.ds(pl.multiple_of(mine * quarter, quarter), quarter)]

    def hop(piece, p, step, shard, upward):
        send, recv = (up_send, up_recv) if upward else (down_send, down_recv)
        target = place(piece, shard, mine)
        return pltpu.make_async_remote_copy(
            src_ref=own(piece) if step == 0 else target,
            dst_ref=target,
            send_sem=send.at[step, p],
            recv_sem=recv.at[step, p],
            device_id=above if upward else below,
            device_id_type=MESH,
        )

    def push(piece, p, slot, shard, part, sems, device):
        block = place(piece, shard, part)
        return pltpu.make_async_remote_copy(
            src_ref=block,
            dst_ref=block,
            send_sem=sems[0].at[slot, p],
            recv_sem=sems[1].at[slot, p],
            device_id=device,
            device_id_type=MESH,
        )

    near_sems, far_sems, on_sems = (sib_send, sib_recv), (far_send, far_recv), (on_send, on_recv)

    def hand_on(step, p, piece):
        for upward in (True, False):
            shard = me - step if upward else me + step
            held = (shard >= 0) if upward else (shard < shards_total)
            slot = (step - 1) * 2 + (0 if upward else 1)

            @pl.when(held)
            def _():
                push(piece, p, slot, shard, theirs, far_sems, across).wait_recv()
                push(piece, p, slot, shard, theirs, on_sems, sibling).start()

    locals_ = [
        pltpu.make_async_copy(
            wqkv_ref, qkv_out.at[pl.ds(pl.multiple_of(me * rows, rows), rows)], local.at[0]
        ),
        pltpu.make_async_copy(
            wproj_ref, proj_out.at[pl.ds(pl.multiple_of(me * rows, rows), rows)], local.at[1]
        ),
        pltpu.make_async_copy(net_ref, net_out.at[me], local.at[2]),
    ]
    steps = shards_total - 1
    for step in range(steps + 1):
        for p, piece in enumerate(pieces):
            for upward in (True, False):
                sign = -1 if upward else 1
                shard = me + sign * step
                held = (shard >= 0) if upward else (shard < shards_total)
                further = has_above if upward else has_below
                if step > 0:
                    slot = (step - 1) * 2 + (0 if upward else 1)

                    @pl.when(held)
                    def _():
                        hop(piece, p, step - 1, shard, upward).wait_recv()
                        if piece != "net":
                            push(piece, p, slot, shard, mine, far_sems, across).start()
                            push(piece, p, slot, shard, mine, near_sems, sibling).start()

                if step < steps:

                    @pl.when(held & further)
                    def _():
                        hop(piece, p, step, shard, upward).start()

            if step > 1 and piece != "net":
                hand_on(step - 1, p, piece)

        if step == 0:
            for copy in locals_:
                copy.start()
    for p, piece in enumerate(pieces):
        if piece != "net":
            hand_on(steps, p, piece)
    for step in range(steps + 1):
        for p, piece in enumerate(pieces):
            for upward in (True, False):
                sign = -1 if upward else 1
                shard = me + sign * step
                held = (shard >= 0) if upward else (shard < shards_total)
                further = has_above if upward else has_below
                if step > 0 and piece != "net":
                    slot = (step - 1) * 2 + (0 if upward else 1)

                    @pl.when(held)
                    def _():
                        beside = side * 2 + 1 - core
                        push(piece, p, slot, shard, mine, far_sems, across).wait_send()
                        push(piece, p, slot, shard, mine, near_sems, sibling).wait_send()
                        push(piece, p, slot, shard, theirs, on_sems, sibling).wait_send()
                        push(piece, p, slot, shard, beside, near_sems, sibling).wait_recv()
                        crossed = (1 - side) * 2 + 1 - core
                        push(piece, p, slot, shard, crossed, on_sems, sibling).wait_recv()

                if step < steps:

                    @pl.when(held & further)
                    def _():
                        hop(piece, p, step, shard, upward).wait_send()

    for copy in locals_:
        copy.wait()


def gather_weights(qkv_weight, proj_weight, net):
    total = lax.axis_size("fsdp")
    rows, width = proj_weight.shape
    pieces = 3
    anywhere = pl.BlockSpec(memory_space=pl.ANY)
    dma = pltpu.SemaphoreType.DMA
    return pl.pallas_call(
        functools.partial(gather_kernel, total),
        out_shape=(
            jax.ShapeDtypeStruct((total * rows, qkv_weight.shape[1]), BF16),
            jax.ShapeDtypeStruct((total * rows, width), BF16),
            jax.ShapeDtypeStruct((total,) + net.shape, F32),
        ),
        in_specs=[anywhere] * 3,
        out_specs=(anywhere,) * 3,
        scratch_shapes=[dma((total - 1, pieces)) for _ in range(4)]
        + [dma((2 * (total - 1), pieces)) for _ in range(6)]
        + [dma((3,))],
        compiler_params=pltpu.CompilerParams(collective_id=0, has_side_effects=True),
        name="gather_weights",
    )(qkv_weight, proj_weight, net)


def expert_kernel(chips, held, capp, *refs):
    normed_ref, routes_ref, slots_ref, win_any, wout_any, ret_ref = refs[:6]
    packed, arrived, answers, win, wout = refs[6:11]
    load, out_send, out_recv, back_send, back_recv, keep = refs[11:]
    rank = lax.axis_index("expert")
    chip, core = rank // 2, lax.rem(rank, 2)

    def rank_of(offset, which):
        return lax.rem(chip + offset, chips) * 2 + which

    barrier = pltpu.get_barrier_semaphore()
    for offset in range(1, 2 * chips):
        other = lax.rem(rank + offset, 2 * chips)
        pl.semaphore_signal(barrier, inc=1, device_id={"expert": other}, device_id_type=MESH)

    loads = []
    for e in range(held):
        loads.append(
            (
                pltpu.make_async_copy(win_any.at[e], win.at[e], load.at[2 * e]),
                pltpu.make_async_copy(wout_any.at[e], wout.at[e], load.at[2 * e + 1]),
            )
        )
        loads[e][0].start()
        loads[e][1].start()

    tokens = normed_ref.shape[0]
    spot = lax.broadcasted_iota(jnp.int32, (capp, tokens), 0)

    def pack(expert):
        hit = (spot == slots_ref[...]) & (routes_ref[...] == expert)
        return dot(jnp.where(hit, 1.0, 0.0).astype(BF16), normed_ref[...]).astype(BF16)

    def spread(k, which, e):
        far = (chips - k) % chips
        target = rank_of(k, which)
        return pltpu.make_async_remote_copy(
            src_ref=packed.at[target * held + e],
            dst_ref=arrived.at[far, e, core],
            send_sem=out_send.at[k, which, e],
            recv_sem=out_recv.at[far, core, e],
            device_id={"expert": target},
            device_id_type=MESH,
        )

    def spread_arrival(k, which, e):
        target = rank_of(k, which)
        return pltpu.make_async_remote_copy(
            src_ref=packed.at[target * held + e],
            dst_ref=arrived.at[k, e, which],
            send_sem=out_send.at[k, which, e],
            recv_sem=out_recv.at[k, which, e],
            device_id={"expert": target},
            device_id_type=MESH,
        )

    def back(k, which, e):
        target = rank_of(k, which)
        return pltpu.make_async_remote_copy(
            src_ref=answers.at[k, e, which],
            dst_ref=ret_ref.at[rank * held + e],
            send_sem=back_send.at[k, which, e],
            recv_sem=back_recv.at[(chips - k) % chips, core, e],
            device_id={"expert": target},
            device_id_type=MESH,
        )

    def back_arrival(k, which, e):
        target = rank_of(k, which)
        return pltpu.make_async_remote_copy(
            src_ref=answers.at[k, e, which],
            dst_ref=ret_ref.at[target * held + e],
            send_sem=back_send.at[k, which, e],
            recv_sem=back_recv.at[k, which, e],
            device_id={"expert": target},
            device_id_type=MESH,
        )

    def partners(k):
        return (0, 1) if k else (1 - core,)

    first = True
    for k in list(range(1, chips)) + [0]:
        for e in range(held):
            for which in partners(k):
                expert = rank_of(k, which) * held + e
                packed[expert] = pack(expert)
                if first:
                    pl.semaphore_wait(barrier, 2 * chips - 1)
                    first = False
                spread(k, which, e).start()
    for e in range(held):
        arrived[0, e, core] = pack(rank * held + e)

    ff = win.shape[2]
    chunk = 512
    for k in range(chips):
        for e in range(held):
            if k == 0:
                loads[e][0].wait()
                loads[e][1].wait()
            for which in partners(k):
                spread_arrival(k, which, e).wait_recv()
            x = arrived[k, e].reshape(2 * capp, arrived.shape[-1])
            total = None
            for f in range(0, ff, chunk):
                inner = dot(x, win[e, :, f : f + chunk])
                inner = (0.5 * inner * (1.0 + lax.erf(inner * math.sqrt(0.5)))).astype(BF16)
                part = dot(inner, wout[e, f : f + chunk, :])
                total = part if total is None else total + part
            answers[k, e] = total.astype(BF16).reshape(2, capp, arrived.shape[-1])
            for which in partners(k):
                back(k, which, e).start()
            if k == 0:
                pltpu.make_async_copy(
                    answers.at[0, e, core], ret_ref.at[rank * held + e], keep.at[e]
                ).start()
    for k in range(chips):
        for e in range(held):
            for which in partners(k):
                spread(k, which, e).wait_send()
                back(k, which, e).wait_send()
                back_arrival(k, which, e).wait_recv()
    for e in range(held):
        pltpu.make_async_copy(
            answers.at[0, e, core], ret_ref.at[rank * held + e], keep.at[e]
        ).wait()


def run_experts(normed, routes, slot_ids, expert_in, expert_out, experts, capp):
    rows, width = normed.shape
    held, _, ff = expert_in.shape
    chips = lax.axis_size("expert") // 2
    anywhere = pl.BlockSpec(memory_space=pl.ANY)
    near = pl.BlockSpec(memory_space=pltpu.VMEM)
    dma = pltpu.SemaphoreType.DMA
    return pl.pallas_call(
        functools.partial(expert_kernel, chips, held, capp),
        out_shape=jax.ShapeDtypeStruct((experts, capp, width), BF16),
        in_specs=[near, near, near, anywhere, anywhere],
        out_specs=anywhere,
        scratch_shapes=[
            pltpu.VMEM((experts, capp, width), BF16),
            pltpu.VMEM((chips, held, 2, capp, width), BF16),
            pltpu.VMEM((chips, held, 2, capp, width), BF16),
            pltpu.VMEM((held, width, ff), BF16),
            pltpu.VMEM((held, ff, width), BF16),
            dma((2 * held,)),
            dma((chips, 2, held)),
            dma((chips, 2, held)),
            dma((chips, 2, held)),
            dma((chips, 2, held)),
            dma((held,)),
        ],
        compiler_params=pltpu.CompilerParams(
            collective_id=1, has_side_effects=True, vmem_limit_bytes=60 * MIB
        ),
        name="experts",
    )(normed, routes.reshape(1, rows), slot_ids.reshape(1, rows), expert_in, expert_out)


def shards(
    tokens, routes, slot_ids, qkv_weight, proj_weight, logit_scale, first_weight, first_offset,
    second_weight, attn_gain, router, moe_gain, expert_in, expert_out,
):
    rows, width = tokens.shape
    units = first_weight.shape[1]
    net = jnp.concatenate(
        [second_weight.T, first_weight, first_offset[None], jnp.zeros((5, units), F32)], axis=0
    )
    wqkv, wproj, net = gather_weights(qkv_weight, proj_weight, net)
    residual, normed = attention(tokens, wqkv, wproj, net, logit_scale, attn_gain, moe_gain)
    experts = router.shape[1]
    cap = rows * 5 // (4 * experts)
    capp = (cap + 15) // 16 * 16
    returned = run_experts(normed, routes, slot_ids, expert_in, expert_out, experts, capp)
    returned = returned.reshape(experts * capp, width)
    return combine(residual, normed, router.T, routes, slot_ids, returned, capp)


def solution(mesh):
    rows = P(("groups", "expert", "fsdp"))
    return jax.shard_map(
        shards,
        mesh=mesh,
        in_specs=(
            P(("groups", "expert", "fsdp"), None), rows, rows, P("fsdp", None), P("fsdp", None),
            P(), P(None, "fsdp"), P("fsdp"), P("fsdp", None), P(), P(), P(),
            P("expert", None, None), P("expert", None, None),
        ),
        out_specs=P(("groups", "expert", "fsdp"), None),
        check_vma=False,
    )
```
